32 devices in a mesh: section: 8 (over y, x, core), dp: 4 (over z).
Axes of the slice: x: 2, y: 2, z: 4, core: 2. Of those that a mesh axis runs over, the one named last changes fastest.
Arguments:
- inputs: bfloat16 [4096, 8192], P(('section', 'dp')), may hold values from -6 to 6
- hidden_grad: bfloat16 [4096, 1024], P(('section', 'dp')), may hold values from -12 to 12
- gate_pre: bfloat16 [4096, 1024], P(('section', 'dp')), may hold values from -8 to 8
- up_weight: bfloat16 [65536, 1024], P(('section', 'dp')), may hold values from -0.1875 to 0.1875
- row_state: float32 [65536], P(('section', 'dp')), may hold values from 100 to 3000
- col_state: float32 [8192], P('section'), may hold values from 100 to 3000
Outputs:
- upstream: bfloat16 [4096, 8192], P(('section', 'dp'))
- param_step: bfloat16 [65536, 1024], P(('section', 'dp'))
- row_out: float32 [65536], P(('section', 'dp'))
- col_out: float32 [8192], P('section')
The draws below stay inside these ranges and needn't reach their ends.
All inputs are finite; a program needn't handle non-finite values.
Results may differ from the reference program's by a relative error of at most 0.0049.
Values may be sent and summed in bfloat16 or wider, within the bound.
No kernel may reach another device: no remote copies, remote signals or barrier semaphores. Data moves between devices by JAX's collectives and lax.ppermute only.
A program may use at most 128 MiB of HBM per device.

```python
import math
import jax
import jax.numpy as jnp
from jax import lax

D = 8192
FF = 1024
TOKENS = 512
N_SECTION = 8


def block_scale(rng, extent, cuts, smallest, high):
    level = 1.0
    for axis_at, shards_of in cuts:
        steps = jax.random.uniform(jax.random.fold_in(jax.random.fold_in(rng, 6), axis_at), (shards_of,), jnp.float32, smallest / len(cuts), high / len(cuts))
        level = level * jnp.repeat(jnp.exp(steps), extent[axis_at] // shards_of).reshape((-1,) + (1,) * (len(extent) - 1 - axis_at))
    return level


def scatter_about(own_key, extent, deviation, most, pieces=(), kind=jnp.bfloat16):
    values = jax.random.normal(own_key, extent, jnp.float32) * deviation
    if len(pieces) > 0:
        values = block_scale(own_key, extent, pieces, -0.22, 0.18) * values
    return jnp.clip(values, min=-most, max=most).astype(kind)


def setup_inputs(seed: int = 0) -> dict:
    key_of = jax.random.split(jax.random.key(seed), 7)
    inputs = scatter_about(key_of[0], (N_SECTION * TOKENS, D), 1.0, 6.0, ((0, 32),))
    hidden_grad = scatter_about(key_of[1], (N_SECTION * TOKENS, FF), 2.0, 12.0, ((0, 32),))
    gate_pre = scatter_about(key_of[2], (N_SECTION * TOKENS, FF), 1.5, 8.0, ((0, 32),))
    up_weight = scatter_about(key_of[3], (N_SECTION * D, FF), FF ** -0.5, 0.1875, ((0, 32),))
    row_state = jnp.clip(jnp.exp(math.log(3000.0) - 3.4011974 * jax.random.uniform(key_of[4], (N_SECTION * D,), jnp.float32) ** block_scale(key_of[4], (N_SECTION * D,), ((0, 32),), -0.2, 0.2)), 100.0, 3000.0)
    col_state = jnp.clip(jnp.exp(math.log(3000.0) - 3.4011974 * jax.random.uniform(key_of[5], (N_SECTION * FF,), jnp.float32) ** block_scale(key_of[5], (N_SECTION * FF,), ((0, 8),), -0.2, 0.2)), 100.0, 3000.0)
    return dict(inputs=inputs, hidden_grad=hidden_grad, gate_pre=gate_pre, up_weight=up_weight, row_state=row_state, col_state=col_state)


BETA_TWO = 0.75
TINY_ADD = 1e-30

def adafactor(gradient, row_state, col_state):
    squares = gradient * gradient + TINY_ADD
    row_new = BETA_TWO * row_state + (1.0 - BETA_TWO) * lax.optimization_barrier(jnp.mean(squares, axis=1))
    col_new = BETA_TWO * col_state + (1.0 - BETA_TWO) * lax.optimization_barrier(jnp.mean(squares, axis=0))
    second = row_new[:, None] * col_new[None, :] / jnp.mean(row_new)
    update = gradient / jnp.sqrt(second)
    root_mean = jnp.sqrt(jnp.mean(update * update))
    step_out = (update / jnp.maximum(1.0, root_mean)).astype(jnp.bfloat16)
    return (step_out, row_new, col_new)

def one_section(operands):
    inputs, hidden_grad, gate_pre, weight, row_state, col_state = operands
    cotangent = (hidden_grad.astype(jnp.float32) * jax.nn.silu(gate_pre.astype(jnp.float32))).astype(jnp.bfloat16)
    lowered = jnp.dot(cotangent, weight.T, preferred_element_type=jnp.float32).astype(jnp.bfloat16)
    gradient = jnp.dot(inputs.T, cotangent, preferred_element_type=jnp.float32)
    step_out, row_new, col_new = adafactor(gradient, row_state, col_state)
    return (lowered, step_out, row_new, col_new)

def reference(inputs, hidden_grad, gate_pre, up_weight, row_state, col_state):
    stacked = (inputs.reshape(N_SECTION, TOKENS, D), hidden_grad.reshape(N_SECTION, TOKENS, FF), gate_pre.reshape(N_SECTION, TOKENS, FF), up_weight.reshape(N_SECTION, D, FF), row_state.reshape(N_SECTION, D), col_state.reshape(N_SECTION, FF))
    lowered, step_out, row_new, col_new = lax.map(one_section, stacked)
    upstream = jnp.concatenate([lowered[1:], jnp.zeros((1, TOKENS, D), jnp.bfloat16)], axis=0)
    return (upstream.reshape(N_SECTION * TOKENS, D), step_out.reshape(N_SECTION * D, FF), row_new.reshape(N_SECTION * D), col_new.reshape(N_SECTION * FF))
```

```python
import functools

import jax
import jax.numpy as jnp
from jax import lax
from jax.experimental import pallas as pl
from jax.experimental.pallas import tpu as pltpu
from jax.sharding import PartitionSpec as P

BETA_TWO = 0.75
TINY_ADD = 1e-30
SECTION, DP = "section", "dp"


def after(value, *others):
    return lax.optimization_barrier((value, *others))[0]


def ring(value, steps):
    count = lax.axis_size(DP)
    return lax.ppermute(value, DP, [(i, (i + steps) % count) for i in range(count)])


def hop(value, origin, steps):
    count = lax.axis_size(DP)
    if steps > 0:
        pairs = [(i, i + 1) for i in range(origin, count - 1)]
    else:
        pairs = [(i, i - 1) for i in range(1, count - origin)]
    return lax.ppermute(value, DP, pairs)


def hand_over(value, steps):
    count, sections = lax.axis_size(DP), lax.axis_size(SECTION)
    pairs = [
        (s * count + i, (s - 1) * count + (i + steps) % count)
        for s in range(1, sections)
        for i in range(count)
    ]
    return lax.ppermute(value, (SECTION, DP), pairs)


def gradient_kernel(parts, entries_per_row, *refs):
    xs, cs = refs[:parts], refs[parts : 2 * parts]
    state_ref, grad_ref, row_ref, col_ref, weighted_ref = refs[2 * parts :]
    step = pl.program_id(0)
    x = jnp.concatenate([r[...] for r in xs], axis=0)
    c = jnp.concatenate([r[...] for r in cs], axis=0)
    grad = lax.dot_general(
        x, c, (((0,), (0,)), ((), ())), preferred_element_type=jnp.float32
    )
    grad_ref[...] = grad
    plain = grad * grad
    squares = plain + TINY_ADD
    row = BETA_TWO * state_ref[...] + (1.0 - BETA_TWO) * (
        jnp.sum(squares, axis=1, keepdims=True) / entries_per_row
    )
    row_ref[...] = row

    @pl.when(step == 0)
    def _():
        col_ref[...] = jnp.zeros_like(col_ref)
        weighted_ref[...] = jnp.zeros_like(weighted_ref)

    col_ref[...] += jnp.sum(squares, axis=0, keepdims=True)
    weighted_ref[...] += jnp.sum(plain / row, axis=0, keepdims=True)


def gradient_call(xs, cs, row_state, block=256):
    parts = len(xs)
    tokens, rows = xs[0].shape
    units = cs[0].shape[1]
    block = min(block, rows)
    return pl.pallas_call(
        functools.partial(gradient_kernel, parts, float(units)),
        grid=(rows // block,),
        in_specs=[pl.BlockSpec((tokens, block), lambda i: (0, i))] * parts
        + [pl.BlockSpec((tokens, units), lambda i: (0, 0))] * parts
        + [pl.BlockSpec((block, 1), lambda i: (i, 0))],
        out_specs=[
            pl.BlockSpec((block, units), lambda i: (i, 0)),
            pl.BlockSpec((block, 1), lambda i: (i, 0)),
            pl.BlockSpec((1, units), lambda i: (0, 0)),
            pl.BlockSpec((1, units), lambda i: (0, 0)),
        ],
        out_shape=[
            jax.ShapeDtypeStruct((rows, units), jnp.float32),
            jax.ShapeDtypeStruct((rows, 1), jnp.float32),
            jax.ShapeDtypeStruct((1, units), jnp.float32),
            jax.ShapeDtypeStruct((1, units), jnp.float32),
        ],
        compiler_params=pltpu.CompilerParams(vmem_limit_bytes=32 * 1024 * 1024),
        cost_estimate=pl.CostEstimate(
            flops=2 * parts * tokens * rows * units,
            bytes_accessed=parts * tokens * (rows + units) * 2 + rows * units * 4,
            transcendentals=0,
        ),
        name="gradient_and_sums",
    )(*xs, *cs, row_state[:, None])


def local(inputs, hidden_grad, gate_pre, up_weight, row_state, col_state):
    count = lax.axis_size(DP)
    me = lax.axis_index(DP)
    tokens, width = inputs.shape
    rows, units = up_weight.shape

    def columns_of(owner):
        return lax.dynamic_slice_in_dim(inputs, owner * rows, rows, axis=1)

    def lowered(cot):
        return lax.dot_general(
            cot, up_weight, (((1,), (1,)), ((), ())), preferred_element_type=jnp.float32
        ).astype(jnp.bfloat16)

    cotangent = (
        hidden_grad.astype(jnp.float32) * jax.nn.silu(gate_pre.astype(jnp.float32))
    ).astype(jnp.bfloat16)

    ahead, behind = {0: cotangent}, {0: cotangent}
    for j in range(1, count):
        ahead[j] = hop(ahead[j - 1], j - 1, 1)
        behind[j] = hop(behind[j - 1], j - 1, -1)
    cots = [cotangent] + [
        jnp.where(me >= k, ahead[k], behind[count - k]) for k in range(1, count)
    ]
    xs = [columns_of(me)] + [
        ring(columns_of(lax.rem(me + k, count)), k) for k in range(1, count)
    ]

    grad, row_new, col_sum, weighted = gradient_call(xs, cots, row_state)
    row_new = row_new[:, 0]
    sums = jnp.concatenate(
        [col_sum[0], weighted[0], jnp.full((units,), jnp.sum(row_new))]
    ).reshape(-1, 128)
    pieces = jnp.stack([sums] + [ring(sums, k) for k in range(1, count)])
    total = jnp.zeros_like(sums)
    for owner in range(count):
        total = total + lax.dynamic_index_in_dim(
            pieces, lax.rem(me - owner + count, count), 0, keepdims=False
        )
    total = total.reshape(3, units)
    row_average = total[2, 0] / width
    col_new = BETA_TWO * col_state + (1.0 - BETA_TWO) * (total[0] / width)
    grand_total = row_average * jnp.sum(total[1] / col_new)
    root_mean = jnp.sqrt(grand_total / (float(width) * float(units)))
    col_factor = lax.rsqrt(col_new) * (jnp.sqrt(row_average) / jnp.maximum(1.0, root_mean))
    step_out = (grad * (lax.rsqrt(row_new)[:, None] * col_factor[None, :])).astype(jnp.bfloat16)

    upstream = jnp.zeros((tokens, width), jnp.bfloat16)
    for k in range(count):
        part = hand_over(lowered(cots[(count - k) % count]), k)
        owner = lax.rem(me - k + count, count)
        upstream = lax.dynamic_update_slice_in_dim(upstream, part, owner * rows, axis=1)
    return (upstream, step_out, row_new, col_new)


def solution(mesh):
    blocks = P((SECTION, DP), None)
    vector = P((SECTION, DP))
    return jax.shard_map(
        local,
        mesh=mesh,
        in_specs=(blocks, blocks, blocks, blocks, vector, P(SECTION)),
        out_specs=(blocks, blocks, vector, P(SECTION)),
        check_vma=False,
    )
```

```python
import functools

import jax
import jax.numpy as jnp
from jax import lax
from jax.experimental import pallas as pl
from jax.experimental.pallas import tpu as pltpu
from jax.sharding import PartitionSpec as P

BETA_TWO = 0.75
TINY_ADD = 1e-30
SECTION, DP = "section", "dp"
MIB = 1024 * 1024
NO_COST = pl.CostEstimate(flops=0, bytes_accessed=0, transcendentals=0)


def after(value, *others):
    return lax.optimization_barrier((value, *others))[0]


def ring(value, steps):
    count = lax.axis_size(DP)
    return lax.ppermute(value, DP, [(i, (i + steps) % count) for i in range(count)])


def reach(value, steps):
    count = lax.axis_size(DP)
    return lax.ppermute(
        value, DP, [(i, i + steps) for i in range(count) if 0 <= i + steps < count]
    )


def hop(value, origin, steps):
    count = lax.axis_size(DP)
    if steps > 0:
        pairs = [(i, i + 1) for i in range(origin, count - 1)]
    else:
        pairs = [(i, i - 1) for i in range(1, count - origin)]
    return lax.ppermute(value, DP, pairs)


def everyone(value):
    count = lax.axis_size(DP)
    if count & (count - 1):
        return lax.psum(value, DP)
    reach_of = 1
    while reach_of < count:
        value = value + lax.ppermute(value, DP, [(i, i ^ reach_of) for i in range(count)])
        reach_of *= 2
    return value


def hand_over(value, steps):
    count, sections = lax.axis_size(DP), lax.axis_size(SECTION)
    pairs = [
        (s * count + i, (s - 1) * count + (i + steps) % count)
        for s in range(1, sections)
        for i in range(count)
    ]
    return lax.ppermute(value, (SECTION, DP), pairs)


def gradient_kernel(parts, sub, *refs):
    xs, cs = refs[:parts], refs[parts : 2 * parts]
    state_ref, scaled_ref, row_ref, sums_ref = refs[2 * parts :]
    block, units = scaled_ref.shape
    c = jnp.concatenate([r[...] for r in cs], axis=0)
    totals = [jnp.zeros((1, units), jnp.float32)] * 2 + [jnp.zeros((1, 1), jnp.float32)]
    for at in range(0, block, sub):
        here = slice(at, at + sub)
        x = jnp.concatenate([r[:, here] for r in xs], axis=0)
        grad = lax.dot_general(
            x, c, (((0,), (0,)), ((), ())), preferred_element_type=jnp.float32
        )
        squares = grad * grad + TINY_ADD
        row = BETA_TWO * state_ref[here, :] + (1.0 - BETA_TWO) * (
            jnp.sum(squares, axis=1, keepdims=True) / float(units)
        )
        scaled = grad * lax.rsqrt(row)
        scaled_ref[here, :] = scaled.astype(scaled_ref.dtype)
        row_ref[:, here] = jnp.broadcast_to(row, (sub, 128)).T[:1, :]
        totals[0] += jnp.sum(squares, axis=0, keepdims=True)
        totals[1] += jnp.sum(scaled * scaled, axis=0, keepdims=True)
        totals[2] += jnp.sum(row, axis=0, keepdims=True)

    @pl.when(pl.program_id(0) == 0)
    def _():
        sums_ref[...] = jnp.zeros_like(sums_ref)

    sums_ref[0:1, :] += totals[0]
    sums_ref[1:2, :] += totals[1]
    sums_ref[2:3, :] += jnp.broadcast_to(totals[2], (1, units))


def gradient_call(xs, cs, row_state, block=1024):
    parts = len(xs)
    tokens, rows = xs[0].shape
    units = cs[0].shape[1]
    block = min(block, rows)
    return pl.pallas_call(
        functools.partial(gradient_kernel, parts, min(256, block)),
        grid=(rows // block,),
        in_specs=[pl.BlockSpec((tokens, block), lambda i: (0, i))] * parts
        + [pl.BlockSpec((tokens, units), lambda i: (0, 0))] * parts
        + [pl.BlockSpec((block, 1), lambda i: (i, 0))],
        out_specs=[
            pl.BlockSpec((block, units), lambda i: (i, 0)),
            pl.BlockSpec((1, block), lambda i: (0, i)),
            pl.BlockSpec((8, units), lambda i: (0, 0)),
        ],
        out_shape=[
            jax.ShapeDtypeStruct((rows, units), jnp.bfloat16),
            jax.ShapeDtypeStruct((1, rows), jnp.float32),
            jax.ShapeDtypeStruct((8, units), jnp.float32),
        ],
        compiler_params=pltpu.CompilerParams(vmem_limit_bytes=24 * MIB),
        cost_estimate=NO_COST,
        name="gradient_and_sums",
    )(*xs, *cs, row_state[:, None])


def step_kernel(width, sums_ref, state_ref, scaled_ref, step_ref, col_ref, factor_ref):
    units = scaled_ref.shape[1]

    @pl.when(pl.program_id(0) == 0)
    def _():
        col = BETA_TWO * state_ref[...] + (1.0 - BETA_TWO) * (sums_ref[0:1, :] / width)
        col_ref[...] = col
        average = sums_ref[2:3, :] / width
        grand = jnp.sum(average * sums_ref[1:2, :] / col, axis=1, keepdims=True)
        root_mean = jnp.sqrt(grand / (width * float(units)))
        factor_ref[...] = lax.rsqrt(col) * jnp.sqrt(average) / jnp.maximum(1.0, root_mean)

    step_ref[...] = (scaled_ref[...] * factor_ref[...]).astype(step_ref.dtype)


def step_call(scaled, sums, col_state, width, block=512):
    rows, units = scaled.shape
    block = min(block, rows)
    return pl.pallas_call(
        functools.partial(step_kernel, float(width)),
        grid=(rows // block,),
        in_specs=[
            pl.BlockSpec((8, units), lambda i: (0, 0)),
            pl.BlockSpec((1, units), lambda i: (0, 0)),
            pl.BlockSpec((block, units), lambda i: (i, 0)),
        ],
        out_specs=[
            pl.BlockSpec((block, units), lambda i: (i, 0)),
            pl.BlockSpec((1, units), lambda i: (0, 0)),
        ],
        out_shape=[
            jax.ShapeDtypeStruct((rows, units), jnp.bfloat16),
            jax.ShapeDtypeStruct((1, units), jnp.float32),
        ],
        scratch_shapes=[pltpu.VMEM((1, units), jnp.float32)],
        compiler_params=pltpu.CompilerParams(vmem_limit_bytes=16 * MIB),
        cost_estimate=NO_COST,
        name="scaled_step",
    )(sums, col_state[None, :], scaled)


def lowered_kernel(cot_ref, weight_ref, out_ref):
    out_ref[...] = lax.dot_general(
        cot_ref[...], weight_ref[...], (((1,), (1,)), ((), ())), preferred_element_type=jnp.float32
    ).astype(out_ref.dtype)


def lowered(cot, weight, block=512):
    tokens, units = cot.shape
    rows = weight.shape[0]
    block = min(block, rows)
    return pl.pallas_call(
        lowered_kernel,
        grid=(rows // block,),
        in_specs=[
            pl.BlockSpec((tokens, units), lambda i: (0, 0)),
            pl.BlockSpec((block, units), lambda i: (i, 0)),
        ],
        out_specs=pl.BlockSpec((tokens, block), lambda i: (0, i)),
        out_shape=jax.ShapeDtypeStruct((tokens, rows), jnp.bfloat16),
        compiler_params=pltpu.CompilerParams(vmem_limit_bytes=16 * MIB),
        cost_estimate=NO_COST,
        name="lowered_block",
    )(cot, weight)


def assemble_kernel(count, me_ref, *refs):
    parts, out_ref = refs[:count], refs[count]
    steps = lax.rem(me_ref[0] - pl.program_id(0) + count, count)
    for k in range(count):
        @pl.when(steps == k)
        def _(k=k):
            out_ref[...] = parts[k][...]


def assemble(parts, me):
    count = len(parts)
    tokens, rows = parts[0].shape
    return pl.pallas_call(
        functools.partial(assemble_kernel, count),
        grid=(count,),
        in_specs=[pl.BlockSpec(memory_space=pltpu.SMEM)]
        + [pl.BlockSpec((tokens, rows), lambda i: (0, 0))] * count,
        out_specs=pl.BlockSpec((tokens, rows), lambda i: (0, i)),
        out_shape=jax.ShapeDtypeStruct((tokens, count * rows), parts[0].dtype),
        compiler_params=pltpu.CompilerParams(vmem_limit_bytes=16 * MIB),
        cost_estimate=NO_COST,
        name="assemble",
    )(me[None], *parts)


def local(inputs, hidden_grad, gate_pre, up_weight, row_state, col_state):
    count = lax.axis_size(DP)
    me = lax.axis_index(DP)
    tokens, width = inputs.shape
    rows, units = up_weight.shape

    def columns_of(owner):
        return lax.dynamic_slice_in_dim(inputs, owner * rows, rows, axis=1)

    cotangent = (
        hidden_grad.astype(jnp.float32) * jax.nn.silu(gate_pre.astype(jnp.float32))
    ).astype(jnp.bfloat16)

    ahead = {1: reach(cotangent, 1), 2: reach(cotangent, 2)}
    behind = {1: reach(cotangent, -1), 2: reach(cotangent, -2)}
    for j in range(3, count):
        ahead[j] = hop(ahead[j - 1], j - 1, 1)
        behind[j] = hop(behind[j - 1], j - 1, -1)
    cots = [cotangent] + [
        jnp.where(me >= k, ahead[k], behind[count - k]) for k in range(1, count)
    ]
    order = list(range(1, count, 2)) + list(range(2, count, 2))
    xs = {}
    for k in order:
        xs[k] = ring(after(columns_of(lax.rem(me + k, count)), cotangent), k)
    xs[0] = after(columns_of(me), ahead[1])
    xs = [xs[k] for k in range(count)]

    low = [lowered(cots[(count - k) % count], up_weight) for k in range(count)]
    sent = [hand_over(low[k], k) for k in range(count)]

    def update(xs, cots, row_state):
        scaled, row_new, sums = gradient_call(xs, cots, row_state)
        return scaled, row_new, everyone(sums)

    def nothing(xs, cots, row_state):
        return (
            jnp.zeros((rows, units), jnp.bfloat16),
            jnp.zeros((1, rows), jnp.float32),
            jnp.zeros((8, units), jnp.float32),
        )

    scaled, row_new, total = lax.cond(
        lax.optimization_barrier(me) < count, update, nothing, xs, cots, row_state
    )
    upstream = assemble([sent[k] for k in range(count)], me)
    step_out, col_new = step_call(scaled, after(total, upstream), col_state, width)
    return (upstream, step_out, row_new.reshape(-1), col_new.reshape(-1))


def solution(mesh):
    blocks = P((SECTION, DP), None)
    vector = P((SECTION, DP))
    return jax.shard_map(
        local,
        mesh=mesh,
        in_specs=(blocks, blocks, blocks, blocks, vector, P(SECTION)),
        out_specs=(blocks, blocks, vector, P(SECTION)),
        check_vma=False,
    )
```

```python
import functools

import jax
import jax.numpy as jnp
from jax import lax
from jax.experimental import pallas as pl
from jax.experimental.pallas import tpu as pltpu
from jax.sharding import PartitionSpec as P

BETA_TWO = 0.75
TINY_ADD = 1e-30
SECTION, DP = "section", "dp"
MIB = 1024 * 1024
NO_COST = pl.CostEstimate(flops=0, bytes_accessed=0, transcendentals=0)


def after(value, *others):
    return lax.optimization_barrier((value, *others))[0]


def partner(steps, index, count):
    return index ^ steps if count & (count - 1) == 0 else (steps - index) % count


def trade(value, steps):
    count = lax.axis_size(DP)
    return lax.ppermute(value, DP, [(i, partner(steps, i, count)) for i in range(count)])


def everyone(value):
    count = lax.axis_size(DP)
    if count & (count - 1):
        return lax.psum(value, DP)
    reach_of = 1
    while reach_of < count:
        value = value + lax.ppermute(value, DP, [(i, i ^ reach_of) for i in range(count)])
        reach_of *= 2
    return value


def hand_over(value, steps):
    count, sections = lax.axis_size(DP), lax.axis_size(SECTION)
    pairs = [
        (s * count + i, (s - 1) * count + partner(steps, i, count))
        for s in range(1, sections)
        for i in range(count)
    ]
    return lax.ppermute(value, (SECTION, DP), pairs)


def gradient_kernel(parts, sub, *refs):
    xs, cs = refs[:parts], refs[parts : 2 * parts]
    state_ref, scaled_ref, row_ref, sums_ref = refs[2 * parts :]
    block, units = scaled_ref.shape
    c = jnp.concatenate([r[...] for r in cs], axis=0)
    totals = [jnp.zeros((1, units), jnp.float32)] * 2 + [jnp.zeros((1, 1), jnp.float32)]
    for at in range(0, block, sub):
        here = slice(at, at + sub)
        x = jnp.concatenate([r[:, here] for r in xs], axis=0)
        grad = lax.dot_general(
            x, c, (((0,), (0,)), ((), ())), preferred_element_type=jnp.float32
        )
        squares = grad * grad + TINY_ADD
        row = BETA_TWO * state_ref[here, :] + (1.0 - BETA_TWO) * (
            jnp.sum(squares, axis=1, keepdims=True) / float(units)
        )
        scaled = grad * lax.rsqrt(row)
        scaled_ref[here, :] = scaled.astype(scaled_ref.dtype)
        row_ref[:, here] = jnp.broadcast_to(row, (sub, 128)).T[:1, :]
        totals[0] += jnp.sum(squares, axis=0, keepdims=True)
        totals[1] += jnp.sum(scaled * scaled, axis=0, keepdims=True)
        totals[2] += jnp.sum(row, axis=0, keepdims=True)

    @pl.when(pl.program_id(0) == 0)
    def _():
        sums_ref[...] = jnp.zeros_like(sums_ref)

    sums_ref[0:1, :] += totals[0]
    sums_ref[1:2, :] += totals[1]
    sums_ref[2:3, :] += jnp.broadcast_to(totals[2], (1, units))


def gradient_call(xs, cs, row_state, block=1024):
    parts = len(xs)
    tokens, rows = xs[0].shape
    units = cs[0].shape[1]
    block = min(block, rows)
    return pl.pallas_call(
        functools.partial(gradient_kernel, parts, min(256, block)),
        grid=(rows // block,),
        in_specs=[pl.BlockSpec((tokens, block), lambda i: (0, i))] * parts
        + [pl.BlockSpec((tokens, units), lambda i: (0, 0))] * parts
        + [pl.BlockSpec((block, 1), lambda i: (i, 0))],
        out_specs=[
            pl.BlockSpec((block, units), lambda i: (i, 0)),
            pl.BlockSpec((1, block), lambda i: (0, i)),
            pl.BlockSpec((8, units), lambda i: (0, 0)),
        ],
        out_shape=[
            jax.ShapeDtypeStruct((rows, units), jnp.float32),
            jax.ShapeDtypeStruct((1, rows), jnp.float32),
            jax.ShapeDtypeStruct((8, units), jnp.float32),
        ],
        compiler_params=pltpu.CompilerParams(vmem_limit_bytes=24 * MIB),
        cost_estimate=NO_COST,
        name="gradient_and_sums",
    )(*xs, *cs, row_state[:, None])


def finish_kernel(
    width, count, me_ref, sums_ref, state_ref, scaled_ref, *refs
):
    parts, (step_ref, col_ref, upstream_ref, factor_ref) = refs[:count], refs[count:]
    units = scaled_ref.shape[1]

    @pl.when(pl.program_id(0) == 0)
    def _():
        col = BETA_TWO * state_ref[...] + (1.0 - BETA_TWO) * (sums_ref[0:1, :] / width)
        col_ref[...] = col
        average = sums_ref[2:3, :] / width
        grand = jnp.sum(average * sums_ref[1:2, :] / col, axis=1, keepdims=True)
        root_mean = jnp.sqrt(grand / (width * float(units)))
        factor_ref[...] = lax.rsqrt(col) * jnp.sqrt(average) / jnp.maximum(1.0, root_mean)

    for k in range(count):
        @pl.when(partner(k, me_ref[0], count) == pl.program_id(0))
        def _(k=k):
            upstream_ref[...] = parts[k][...]

    step_ref[...] = (scaled_ref[...] * factor_ref[...]).astype(step_ref.dtype)


def finish(scaled, sums, col_state, width, parts, me):
    count = len(parts)
    rows, units = scaled.shape
    tokens = parts[0].shape[0]
    block = rows // count
    return pl.pallas_call(
        functools.partial(finish_kernel, float(width), count),
        grid=(count,),
        in_specs=[
            pl.BlockSpec(memory_space=pltpu.SMEM),
            pl.BlockSpec((8, units), lambda i: (0, 0)),
            pl.BlockSpec((1, units), lambda i: (0, 0)),
            pl.BlockSpec((block, units), lambda i: (i, 0)),
        ]
        + [pl.BlockSpec((tokens, rows), lambda i: (0, 0))] * count,
        out_specs=[
            pl.BlockSpec((block, units), lambda i: (i, 0)),
            pl.BlockSpec((1, units), lambda i: (0, 0)),
            pl.BlockSpec((tokens, rows), lambda i: (0, i)),
        ],
        out_shape=[
            jax.ShapeDtypeStruct((rows, units), jnp.bfloat16),
            jax.ShapeDtypeStruct((1, units), jnp.float32),
            jax.ShapeDtypeStruct((tokens, count * rows), parts[0].dtype),
        ],
        scratch_shapes=[pltpu.VMEM((1, units), jnp.float32)],
        compiler_params=pltpu.CompilerParams(vmem_limit_bytes=24 * MIB),
        cost_estimate=NO_COST,
        name="finish",
    )(me[None], sums, col_state[None, :], scaled, *parts)


def lowered_kernel(cot_ref, weight_ref, out_ref):
    out_ref[...] = lax.dot_general(
        cot_ref[...], weight_ref[...], (((1,), (1,)), ((), ())), preferred_element_type=jnp.float32
    ).astype(out_ref.dtype)


def lowered(cot, weight, block=512):
    tokens, units = cot.shape
    rows = weight.shape[0]
    block = min(block, rows)
    return pl.pallas_call(
        lowered_kernel,
        grid=(rows // block,),
        in_specs=[
            pl.BlockSpec((tokens, units), lambda i: (0, 0)),
            pl.BlockSpec((block, units), lambda i: (i, 0)),
        ],
        out_specs=pl.BlockSpec((tokens, block), lambda i: (0, i)),
        out_shape=jax.ShapeDtypeStruct((tokens, rows), jnp.bfloat16),
        compiler_params=pltpu.CompilerParams(vmem_limit_bytes=16 * MIB),
        cost_estimate=NO_COST,
        name="lowered_block",
    )(cot, weight)


def local(inputs, hidden_grad, gate_pre, up_weight, row_state, col_state):
    count = lax.axis_size(DP)
    me = lax.axis_index(DP)
    tokens, width = inputs.shape
    rows, units = up_weight.shape

    def columns_of(owner):
        return lax.dynamic_slice_in_dim(inputs, owner * rows, rows, axis=1)

    cotangent = (
        hidden_grad.astype(jnp.float32) * jax.nn.silu(gate_pre.astype(jnp.float32))
    ).astype(jnp.bfloat16)

    cots, xs = {0: cotangent}, {0: after(columns_of(me), cotangent)}
    if count == 4:
        inner, outward = [(1, 2), (2, 1)], [(1, 0), (2, 3)]
        is_inner = (me == 1) | (me == 2)
        cots[1] = trade(cotangent, 1)
        middle = lax.ppermute(cotangent, DP, inner)
        across = lax.ppermute(cots[1], DP, inner)
        second = lax.ppermute(middle, DP, outward)
        third = lax.ppermute(across, DP, outward)
        cots[2] = jnp.where(is_inner, across, second)
        cots[3] = jnp.where(is_inner, middle, third)
        first, nearest = (across,), (third,)
    else:
        for k in range(1, count):
            cots[k] = trade(cotangent, k)
        first = nearest = (cots[1],)
    for k in range(1, count):
        xs[k] = trade(after(columns_of(partner(k, me, count)), *(first if k > 1 else nearest)), k)
    cots = [cots[k] for k in range(count)]
    xs = [xs[k] for k in range(count)]
    low = [lowered(cots[k], up_weight) for k in range(count)]
    waits = {3: (2, 3)}
    sent = [
        hand_over(after(low[k], *[xs[j] for j in waits.get(k, ())]) if k in waits else low[k], k)
        for k in range(count)
    ]

    def update(xs, cots, row_state):
        scaled, row_new, sums = gradient_call(xs, cots, row_state)
        return scaled, row_new, everyone(sums)

    def nothing(xs, cots, row_state):
        return (
            jnp.zeros((rows, units), jnp.float32),
            jnp.zeros((1, rows), jnp.float32),
            jnp.zeros((8, units), jnp.float32),
        )

    scaled, row_new, total = lax.cond(
        lax.optimization_barrier(me) < count, update, nothing, xs, cots, row_state
    )
    step_out, col_new, upstream = finish(
        scaled, total, col_state, width, [sent[k] for k in range(count)], me
    )
    return (upstream, step_out, row_new.reshape(-1), col_new.reshape(-1))


def solution(mesh):
    blocks = P((SECTION, DP), None)
    vector = P((SECTION, DP))
    return jax.shard_map(
        local,
        mesh=mesh,
        in_specs=(blocks, blocks, blocks, blocks, vector, P(SECTION)),
        out_specs=(blocks, blocks, vector, P(SECTION)),
        check_vma=False,
    )
```

```python
import functools

import jax
import jax.numpy as jnp
from jax import lax
from jax.experimental import pallas as pl
from jax.experimental.pallas import tpu as pltpu
from jax.sharding import PartitionSpec as P

BETA_TWO = 0.75
TINY_ADD = 1e-30
SECTION, DP = "section", "dp"
MIB = 1024 * 1024
NO_COST = pl.CostEstimate(flops=0, bytes_accessed=0, transcendentals=0)


def after(value, *others):
    return lax.optimization_barrier((value, *others))[0]


def partner(steps, index, count):
    return index ^ steps if count & (count - 1) == 0 else (steps - index) % count


def trade(value, steps):
    count = lax.axis_size(DP)
    return lax.ppermute(value, DP, [(i, partner(steps, i, count)) for i in range(count)])


def everyone(value):
    count = lax.axis_size(DP)
    if count & (count - 1):
        return lax.psum(value, DP)
    reach_of = 1
    while reach_of < count:
        value = value + lax.ppermute(value, DP, [(i, i ^ reach_of) for i in range(count)])
        reach_of *= 2
    return value


def hand_over(value, steps):
    count, sections = lax.axis_size(DP), lax.axis_size(SECTION)
    pairs = [
        (s * count + i, (s - 1) * count + partner(steps, i, count))
        for s in range(1, sections)
        for i in range(count)
    ]
    return lax.ppermute(value, (SECTION, DP), pairs)


def gradient_kernel(parts, sub, *refs):
    xs, cs = refs[:parts], refs[parts : 2 * parts]
    state_ref, scaled_ref, row_ref, sums_ref = refs[2 * parts :]
    block, units = scaled_ref.shape
    c = jnp.concatenate([r[...] for r in cs], axis=0)
    totals = [jnp.zeros((1, units), jnp.float32)] * 2 + [jnp.zeros((1, 1), jnp.float32)]
    for at in range(0, block, sub):
        here = slice(at, at + sub)
        x = jnp.concatenate([r[:, here] for r in xs], axis=0)
        grad = lax.dot_general(
            x, c, (((0,), (0,)), ((), ())), preferred_element_type=jnp.float32
        )
        squares = grad * grad + TINY_ADD
        row = BETA_TWO * state_ref[here, :] + (1.0 - BETA_TWO) * (
            jnp.sum(squares, axis=1, keepdims=True) / float(units)
        )
        scaled = grad * lax.rsqrt(row)
        scaled_ref[here, :] = scaled.astype(scaled_ref.dtype)
        row_ref[:, here] = jnp.broadcast_to(row, (sub, 128)).T[:1, :]
        totals[0] += jnp.sum(squares, axis=0, keepdims=True)
        totals[1] += jnp.sum(scaled * scaled, axis=0, keepdims=True)
        totals[2] += jnp.sum(row, axis=0, keepdims=True)

    @pl.when(pl.program_id(0) == 0)
    def _():
        sums_ref[...] = jnp.zeros_like(sums_ref)

    sums_ref[0:1, :] += totals[0]
    sums_ref[1:2, :] += totals[1]
    sums_ref[2:3, :] += jnp.broadcast_to(totals[2], (1, units))


def gradient_call(xs, cs, row_state, block=1024):
    parts = len(xs)
    tokens, rows = xs[0].shape
    units = cs[0].shape[1]
    block = min(block, rows)
    return pl.pallas_call(
        functools.partial(gradient_kernel, parts, min(256, block)),
        grid=(rows // block,),
        in_specs=[pl.BlockSpec((tokens, block), lambda i: (0, i))] * parts
        + [pl.BlockSpec((tokens, units), lambda i: (0, 0))] * parts
        + [pl.BlockSpec((block, 1), lambda i: (i, 0))],
        out_specs=[
            pl.BlockSpec((block, units), lambda i: (i, 0)),
            pl.BlockSpec((1, block), lambda i: (0, i)),
            pl.BlockSpec((8, units), lambda i: (0, 0)),
        ],
        out_shape=[
            jax.ShapeDtypeStruct((rows, units), jnp.float32),
            jax.ShapeDtypeStruct((1, rows), jnp.float32),
            jax.ShapeDtypeStruct((8, units), jnp.float32),
        ],
        compiler_params=pltpu.CompilerParams(vmem_limit_bytes=24 * MIB),
        cost_estimate=NO_COST,
        name="gradient_and_sums",
    )(*xs, *cs, row_state)


def finish_kernel(
    width, count, me_ref, sums_ref, state_ref, scaled_ref, *refs
):
    parts, (step_ref, col_ref, upstream_ref, factor_ref) = refs[:count], refs[count:]
    units = scaled_ref.shape[1]

    @pl.when(pl.program_id(0) == 0)
    def _():
        col = BETA_TWO * state_ref[...] + (1.0 - BETA_TWO) * (sums_ref[0:1, :] / width)
        col_ref[...] = col
        average = sums_ref[2:3, :] / width
        grand = jnp.sum(average * sums_ref[1:2, :] / col, axis=1, keepdims=True)
        root_mean = jnp.sqrt(grand / (width * float(units)))
        factor_ref[...] = lax.rsqrt(col) * jnp.sqrt(average) / jnp.maximum(1.0, root_mean)

    for k in range(count):
        @pl.when(partner(k, me_ref[0], count) == pl.program_id(0))
        def _(k=k):
            upstream_ref[...] = parts[k][...]

    step_ref[...] = (scaled_ref[...] * factor_ref[...]).astype(step_ref.dtype)


def finish(scaled, sums, col_state, width, parts, me):
    count = len(parts)
    rows, units = scaled.shape
    tokens = parts[0].shape[0]
    block = rows // count
    return pl.pallas_call(
        functools.partial(finish_kernel, float(width), count),
        grid=(count,),
        in_specs=[
            pl.BlockSpec(memory_space=pltpu.SMEM),
            pl.BlockSpec((8, units), lambda i: (0, 0)),
            pl.BlockSpec((1, units), lambda i: (0, 0)),
            pl.BlockSpec((block, units), lambda i: (i, 0)),
        ]
        + [pl.BlockSpec((tokens, rows), lambda i: (0, 0))] * count,
        out_specs=[
            pl.BlockSpec((block, units), lambda i: (i, 0)),
            pl.BlockSpec((1, units), lambda i: (0, 0)),
            pl.BlockSpec((tokens, rows), lambda i: (0, i)),
        ],
        out_shape=[
            jax.ShapeDtypeStruct((rows, units), jnp.bfloat16),
            jax.ShapeDtypeStruct((1, units), jnp.float32),
            jax.ShapeDtypeStruct((tokens, count * rows), parts[0].dtype),
        ],
        scratch_shapes=[pltpu.VMEM((1, units), jnp.float32)],
        compiler_params=pltpu.CompilerParams(vmem_limit_bytes=24 * MIB),
        cost_estimate=NO_COST,
        name="finish",
    )(me[None], sums, col_state[None, :], scaled, *parts)


def lowered_kernel(cot_ref, weight_ref, out_ref):
    out_ref[...] = lax.dot_general(
        cot_ref[...], weight_ref[...], (((1,), (1,)), ((), ())), preferred_element_type=jnp.float32
    ).astype(out_ref.dtype)


def lowered(cot, weight, block=512):
    tokens, units = cot.shape
    rows = weight.shape[0]
    block = min(block, rows)
    return pl.pallas_call(
        lowered_kernel,
        grid=(rows // block,),
        in_specs=[
            pl.BlockSpec((tokens, units), lambda i: (0, 0)),
            pl.BlockSpec((block, units), lambda i: (i, 0)),
        ],
        out_specs=pl.BlockSpec((tokens, block), lambda i: (0, i)),
        out_shape=jax.ShapeDtypeStruct((tokens, rows), jnp.bfloat16),
        compiler_params=pltpu.CompilerParams(vmem_limit_bytes=16 * MIB),
        cost_estimate=NO_COST,
        name="lowered_block",
    )(cot, weight)


def local(inputs, hidden_grad, gate_pre, up_weight, row_state, col_state):
    count = lax.axis_size(DP)
    me = lax.axis_index(DP)
    tokens, width = inputs.shape
    rows, units = up_weight.shape

    def columns_of(owner):
        return lax.dynamic_slice_in_dim(inputs, owner * rows, rows, axis=1)

    cotangent = (
        hidden_grad.astype(jnp.float32) * jax.nn.silu(gate_pre.astype(jnp.float32))
    ).astype(jnp.bfloat16)

    row_state = after(row_state[:, None], cotangent)
    cots, xs = {0: cotangent}, {0: after(columns_of(me), cotangent)}
    if count == 4:
        inner, outward = [(1, 2), (2, 1)], [(1, 0), (2, 3)]
        is_inner = (me == 1) | (me == 2)
        cots[1] = trade(cotangent, 1)
        middle = lax.ppermute(cotangent, DP, inner)
        across = lax.ppermute(cots[1], DP, inner)
        second = lax.ppermute(middle, DP, outward)
        third = lax.ppermute(across, DP, outward)
        cots[2] = jnp.where(is_inner, across, second)
        cots[3] = jnp.where(is_inner, middle, third)
        first, nearest = (across,), (third,)
    else:
        for k in range(1, count):
            cots[k] = trade(cotangent, k)
        first = nearest = (cots[1],)
    for k in range(1, count):
        xs[k] = trade(after(columns_of(partner(k, me, count)), *(first if k > 1 else nearest)), k)
    cots = [cots[k] for k in range(count)]
    xs = [xs[k] for k in range(count)]
    low = [lowered(cots[k], up_weight) for k in range(count)]
    waits = {0: (2,), 3: (2, 3)}
    sent = [
        hand_over(after(low[k], *[xs[j] for j in waits.get(k, ())]) if k in waits else low[k], k)
        for k in range(count)
    ]

    def update(xs, cots, row_state):
        scaled, row_new, sums = gradient_call(xs, cots, row_state)
        return scaled, row_new, everyone(sums)

    def nothing(xs, cots, row_state):
        return (
            jnp.zeros((rows, units), jnp.float32),
            jnp.zeros((1, rows), jnp.float32),
            jnp.zeros((8, units), jnp.float32),
        )

    scaled, row_new, total = lax.cond(
        lax.optimization_barrier(me) < count, update, nothing, xs, cots, row_state
    )
    step_out, col_new, upstream = finish(
        scaled, total, col_state, width, [sent[k] for k in range(count)], me
    )
    return (upstream, step_out, row_new.reshape(-1), col_new.reshape(-1))


def solution(mesh):
    blocks = P((SECTION, DP), None)
    vector = P((SECTION, DP))
    return jax.shard_map(
        local,
        mesh=mesh,
        in_specs=(blocks, blocks, blocks, blocks, vector, P(SECTION)),
        out_specs=(blocks, blocks, vector, P(SECTION)),
        check_vma=False,
    )
```

```python
import functools

import jax
import jax.numpy as jnp
from jax import lax
from jax.experimental import pallas as pl
from jax.experimental.pallas import tpu as pltpu
from jax.sharding import PartitionSpec as P

BETA_TWO = 0.75
TINY_ADD = 1e-30
SECTION, DP = "section", "dp"
MIB = 1024 * 1024
NO_COST = pl.CostEstimate(flops=0, bytes_accessed=0, transcendentals=0)


def after(value, *others):
    return lax.optimization_barrier((value, *others))[0]


def partner(steps, index, count):
    return index ^ steps if count & (count - 1) == 0 else (steps - index) % count


def trade(value, steps):
    count = lax.axis_size(DP)
    return lax.ppermute(value, DP, [(i, partner(steps, i, count)) for i in range(count)])


def everyone(value):
    count = lax.axis_size(DP)
    if count & (count - 1):
        return lax.psum(value, DP)
    reach_of = 1
    while reach_of < count:
        value = value + lax.ppermute(value, DP, [(i, i ^ reach_of) for i in range(count)])
        reach_of *= 2
    return value


def hand_over(value, steps):
    count, sections = lax.axis_size(DP), lax.axis_size(SECTION)
    pairs = [
        (s * count + i, (s - 1) * count + partner(steps, i, count))
        for s in range(1, sections)
        for i in range(count)
    ]
    return lax.ppermute(value, (SECTION, DP), pairs)


def gradient_kernel(parts, sub, *refs):
    xs, cs = refs[:parts], refs[parts : 2 * parts]
    state_ref, scaled_ref, row_ref, sums_ref = refs[2 * parts :]
    block, units = scaled_ref.shape
    c = jnp.concatenate([r[...] for r in cs], axis=0)
    totals = [jnp.zeros((1, units), jnp.float32)] * 2 + [jnp.zeros((1, 1), jnp.float32)]
    for at in range(0, block, sub):
        here = slice(at, at + sub)
        x = jnp.concatenate([r[:, here] for r in xs], axis=0)
        grad = lax.dot_general(
            x, c, (((0,), (0,)), ((), ())), preferred_element_type=jnp.float32
        )
        squares = grad * grad + TINY_ADD
        row = BETA_TWO * state_ref[here, :] + (1.0 - BETA_TWO) * (
            jnp.sum(squares, axis=1, keepdims=True) / float(units)
        )
        scaled = grad * lax.rsqrt(row)
        scaled_ref[here, :] = scaled.astype(scaled_ref.dtype)
        row_ref[:, here] = jnp.broadcast_to(row, (sub, 128)).T[:1, :]
        totals[0] += jnp.sum(squares, axis=0, keepdims=True)
        totals[1] += jnp.sum(scaled * scaled, axis=0, keepdims=True)
        totals[2] += jnp.sum(row, axis=0, keepdims=True)

    @pl.when(pl.program_id(0) == 0)
    def _():
        sums_ref[...] = jnp.zeros_like(sums_ref)

    sums_ref[0:1, :] += totals[0]
    sums_ref[1:2, :] += totals[1]
    sums_ref[2:3, :] += jnp.broadcast_to(totals[2], (1, units))


def gradient_call(xs, cs, row_state, block=1024):
    parts = len(xs)
    tokens, rows = xs[0].shape
    units = cs[0].shape[1]
    block = min(block, rows)
    return pl.pallas_call(
        functools.partial(gradient_kernel, parts, min(256, block)),
        grid=(rows // block,),
        in_specs=[pl.BlockSpec((tokens, block), lambda i: (0, i))] * parts
        + [pl.BlockSpec((tokens, units), lambda i: (0, 0))] * parts
        + [pl.BlockSpec((block, 1), lambda i: (i, 0))],
        out_specs=[
            pl.BlockSpec((block, units), lambda i: (i, 0)),
            pl.BlockSpec((1, block), lambda i: (0, i)),
            pl.BlockSpec((8, units), lambda i: (0, 0)),
        ],
        out_shape=[
            jax.ShapeDtypeStruct((rows, units), jnp.float32),
            jax.ShapeDtypeStruct((1, rows), jnp.float32),
            jax.ShapeDtypeStruct((8, units), jnp.float32),
        ],
        compiler_params=pltpu.CompilerParams(vmem_limit_bytes=24 * MIB),
        cost_estimate=NO_COST,
        name="gradient_and_sums",
    )(*xs, *cs, row_state[:, None])


def finish_kernel(
    width, count, me_ref, sums_ref, state_ref, scaled_ref, *refs
):
    parts, (step_ref, col_ref, upstream_ref, factor_ref) = refs[:count], refs[count:]
    units = scaled_ref.shape[1]

    @pl.when(pl.program_id(0) == 0)
    def _():
        col = BETA_TWO * state_ref[...] + (1.0 - BETA_TWO) * (sums_ref[0:1, :] / width)
        col_ref[...] = col
        average = sums_ref[2:3, :] / width
        grand = jnp.sum(average * sums_ref[1:2, :] / col, axis=1, keepdims=True)
        root_mean = jnp.sqrt(grand / (width * float(units)))
        factor_ref[...] = lax.rsqrt(col) * jnp.sqrt(average) / jnp.maximum(1.0, root_mean)

    for k in range(count):
        @pl.when(partner(k, me_ref[0], count) == pl.program_id(0))
        def _(k=k):
            upstream_ref[...] = parts[k][...]

    step_ref[...] = (scaled_ref[...] * factor_ref[...]).astype(step_ref.dtype)


def finish(scaled, sums, col_state, width, parts, me):
    count = len(parts)
    rows, units = scaled.shape
    tokens = parts[0].shape[0]
    block = rows // count
    return pl.pallas_call(
        functools.partial(finish_kernel, float(width), count),
        grid=(count,),
        in_specs=[
            pl.BlockSpec(memory_space=pltpu.SMEM),
            pl.BlockSpec((8, units), lambda i: (0, 0)),
            pl.BlockSpec((1, units), lambda i: (0, 0)),
            pl.BlockSpec((block, units), lambda i: (i, 0)),
        ]
        + [pl.BlockSpec((tokens, rows), lambda i: (0, 0))] * count,
        out_specs=[
            pl.BlockSpec((block, units), lambda i: (i, 0)),
            pl.BlockSpec((1, units), lambda i: (0, 0)),
            pl.BlockSpec((tokens, rows), lambda i: (0, i)),
        ],
        out_shape=[
            jax.ShapeDtypeStruct((rows, units), jnp.bfloat16),
            jax.ShapeDtypeStruct((1, units), jnp.float32),
            jax.ShapeDtypeStruct((tokens, count * rows), parts[0].dtype),
        ],
        scratch_shapes=[pltpu.VMEM((1, units), jnp.float32)],
        compiler_params=pltpu.CompilerParams(vmem_limit_bytes=24 * MIB),
        cost_estimate=NO_COST,
        name="finish",
    )(me[None], sums, col_state[None, :], scaled, *parts)


def lowered_kernel(cot_ref, weight_ref, out_ref):
    out_ref[...] = lax.dot_general(
        cot_ref[...], weight_ref[...], (((1,), (1,)), ((), ())), preferred_element_type=jnp.float32
    ).astype(out_ref.dtype)


def lowered(cot, weight, block=512):
    tokens, units = cot.shape
    rows = weight.shape[0]
    block = min(block, rows)
    return pl.pallas_call(
        lowered_kernel,
        grid=(rows // block,),
        in_specs=[
            pl.BlockSpec((tokens, units), lambda i: (0, 0)),
            pl.BlockSpec((block, units), lambda i: (i, 0)),
        ],
        out_specs=pl.BlockSpec((tokens, block), lambda i: (0, i)),
        out_shape=jax.ShapeDtypeStruct((tokens, rows), jnp.bfloat16),
        compiler_params=pltpu.CompilerParams(vmem_limit_bytes=16 * MIB),
        cost_estimate=NO_COST,
        name="lowered_block",
    )(cot, weight)


def local(inputs, hidden_grad, gate_pre, up_weight, row_state, col_state):
    count = lax.axis_size(DP)
    me = lax.axis_index(DP)
    tokens, width = inputs.shape
    rows, units = up_weight.shape

    def columns_of(owner):
        return lax.dynamic_slice_in_dim(inputs, owner * rows, rows, axis=1)

    cotangent = (
        hidden_grad.astype(jnp.float32) * jax.nn.silu(gate_pre.astype(jnp.float32))
    ).astype(jnp.bfloat16)

    cots, xs = {0: cotangent}, {0: after(columns_of(me), cotangent)}
    if count == 4:
        inner, outward = [(1, 2), (2, 1)], [(1, 0), (2, 3)]
        is_inner = (me == 1) | (me == 2)
        cots[1] = trade(cotangent, 1)
        middle = lax.ppermute(cotangent, DP, inner)
        across = lax.ppermute(cots[1], DP, inner)
        second = lax.ppermute(middle, DP, outward)
        third = lax.ppermute(across, DP, outward)
        cots[2] = jnp.where(is_inner, across, second)
        cots[3] = jnp.where(is_inner, middle, third)
        first, nearest = (across,), (third, second)
    else:
        for k in range(1, count):
            cots[k] = trade(cotangent, k)
        first = nearest = (cots[1],)
    for k in range(1, count):
        xs[k] = trade(after(columns_of(partner(k, me, count)), *(first if k > 1 else nearest)), k)
    cots = [cots[k] for k in range(count)]
    xs = [xs[k] for k in range(count)]
    low = [lowered(cots[k], up_weight) for k in range(count)]
    waits = {3: (2, 3)}
    sent = [
        hand_over(after(low[k], *[xs[j] for j in waits.get(k, ())]) if k in waits else low[k], k)
        for k in range(count)
    ]

    def update(xs, cots, row_state):
        scaled, row_new, sums = gradient_call(xs, cots, row_state)
        return scaled, row_new, everyone(sums)

    def nothing(xs, cots, row_state):
        return (
            jnp.zeros((rows, units), jnp.float32),
            jnp.zeros((1, rows), jnp.float32),
            jnp.zeros((8, units), jnp.float32),
        )

    scaled, row_new, total = lax.cond(
        lax.optimization_barrier(me) < count, update, nothing, xs, cots, row_state
    )
    step_out, col_new, upstream = finish(
        scaled, total, col_state, width, [sent[k] for k in range(count)], me
    )
    return (upstream, step_out, row_new.reshape(-1), col_new.reshape(-1))


def solution(mesh):
    blocks = P((SECTION, DP), None)
    vector = P((SECTION, DP))
    return jax.shard_map(
        local,
        mesh=mesh,
        in_specs=(blocks, blocks, blocks, blocks, vector, P(SECTION)),
        out_specs=(blocks, blocks, vector, P(SECTION)),
        check_vma=False,
    )
```
